32 devices in a mesh: req: 32 (over z, y, x, core), mlp: 1.
Axes of the slice: x: 2, y: 2, z: 4, core: 2. Of those that a mesh axis runs over, the one named last changes fastest.
Arguments:
- tokens: bfloat16 [12288, 2048], P(('req', 'mlp')), may hold values from -6 to 6
- lengths: int32 [4], replicated, may hold values from 1 to 6144, 12288 in all
- in_gain: float32 [2048], replicated, may hold values from 0.5 to 1.5
- w_query: bfloat16 [2048, 2048], P(None, 'mlp'), may hold values from -0.125 to 0.125
- w_key: bfloat16 [2048, 2048], P(None, 'mlp'), may hold values from -1 to 1
- w_value: bfloat16 [2048, 4096], P(None, 'mlp'), may hold values from -0.125 to 0.125
- w_gate: bfloat16 [2048, 4096], P(None, 'mlp'), may hold values from -0.125 to 0.125
- w_beta: bfloat16 [2048, 16], P(None, 'mlp'), may hold values from -0.125 to 0.125
- w_decay: bfloat16 [2048, 16], P(None, 'mlp'), may hold values from -0.125 to 0.125
- decay_log: float32 [16], P('mlp'), may hold values from -11 to 0
- decay_bias: float32 [16], P('mlp'), may hold values from -3 to 1
- conv_query: float32 [4, 2048], P(None, 'mlp'), may hold values from -2.5 to 2.5
- conv_key: float32 [4, 2048], P(None, 'mlp'), may hold values from -2.5 to 2.5
- conv_value: float32 [4, 4096], P(None, 'mlp'), may hold values from -2.5 to 2.5
- head_gain: float32 [256], replicated, may hold values from 0.5 to 1.5
- w_out: bfloat16 [4096, 2048], P('mlp'), may hold values from -0.09375 to 0.09375
- mlp_gain: float32 [2048], replicated, may hold values from 0.5 to 1.5
- w_up_gate: bfloat16 [2048, 5632], P('req', 'mlp'), may hold values from -0.125 to 0.125
- w_up: bfloat16 [2048, 5632], P('req', 'mlp'), may hold values from -0.125 to 0.125
- w_down: bfloat16 [5632, 2048], P('mlp', 'req'), may hold values from -0.078125 to 0.078125
Outputs:
- layer_out: bfloat16 [12288, 2048], P(('req', 'mlp'))
The draws below stay inside these ranges and needn't reach their ends.
Inputs may be any that keep to these rules, and one draw needn't show every extreme that they name: The 4 prompts lie end to end in the order given and their lengths sum to 12288; the longest has exactly 6144 tokens.
All inputs are finite; a program needn't handle non-finite values.
Results may differ from the reference program's by a relative error of at most 0.017.
Values may be sent and summed in bfloat16 or wider, within the bound.
A program may use at most 384 MiB of HBM per device.

```python
import math
import jax
import jax.numpy as jnp
import numpy as np
from jax import lax

D = 2048
HEADS = 16
DK = 128
DV = 256
FF = 5632
CONV = 4
GROUP = 64
PROMPTS = 4
TOKENS = 12288
LONGEST = 6144


def slow_heads(key, slow_count):
    ranking = jax.random.permutation(jax.random.fold_in(key, 101), HEADS)
    return ranking < slow_count


def draw_decay_log(key, part):
    slow_count = HEADS // 2
    lower_factor = 1.0
    upper_factor = 4.0
    slow_mask = slow_heads(key, slow_count)
    reach_factor = jax.random.uniform(jax.random.fold_in(key, 102), (HEADS,), jnp.float32, lower_factor, upper_factor)
    slow_value = jnp.log(reach_factor / LONGEST)
    fast_value = jax.random.uniform(jax.random.fold_in(key, 103), (HEADS,), jnp.float32, -3.0, 0.0)
    return jnp.where(slow_mask, slow_value, fast_value).astype(jnp.float32)


def draw_decay_bias(key, part):
    slow_count = HEADS // 2
    slow_mask = slow_heads(key, slow_count)
    slow_value = jax.random.uniform(jax.random.fold_in(key, 104), (HEADS,), jnp.float32, -3.0, -2.0)
    fast_value = jax.random.uniform(jax.random.fold_in(key, 105), (HEADS,), jnp.float32, -1.0, 1.0)
    return jnp.where(slow_mask, slow_value, fast_value).astype(jnp.float32)


def draw_w_key(key, part):
    column_scale = jnp.exp(jax.random.uniform(jax.random.fold_in(key, 111), (HEADS * DK,), jnp.float32, -3.0, 0.0))
    entries = jax.random.truncated_normal(jax.random.fold_in(key, 112), -6.0, 6.0, (D, HEADS * DK), jnp.float32)
    return (entries * D ** (-0.5) * column_scale[None, :]).astype(jnp.bfloat16)


def block_levels(own_key, extent, shards, least, largest):
    def one(dim, shards_of):
        steps = jax.random.uniform(jax.random.fold_in(jax.random.fold_in(own_key, 6), dim), (shards_of,), jnp.float32, least / len(shards), largest / len(shards))
        return jnp.repeat(jnp.exp(steps), extent[dim] // shards_of).reshape((-1,) + (1,) * (len(extent) - dim - 1))

    level = one(*shards[0])
    for cut in shards[1:]:
        level = level * one(*cut)
    return level


def length_profile(count, total, limit, slope):
    loads = [(1 << 20) // math.isqrt(rank ** slope) + 1 for rank in range(2, count + 1)]
    rest, counts = total - limit - (count - 1), [1] * (count - 1)
    while rest > 0:
        candidates = [i for i in range(count - 1) if counts[i] < limit]
        whole, budget = sum([loads[i] for i in candidates]), rest
        for i in candidates:
            more = min(limit - counts[i], max(1, budget * loads[i] // whole), rest)
            counts[i] = counts[i] + more
            rest = rest - more
    return np.array([limit] + counts)


def ragged(stream_key, count, total, limit, skew):
    if count == 2:
        one = jax.random.randint(stream_key, (), max(1, total - limit), min(limit, total - 1) + 1)
        return jnp.stack([one, total - one])
    tallies = jnp.asarray(length_profile(count, total, limit, skew), jnp.int32)
    couples = (count - 1) // 2
    giver, receiver = tallies[1:1 + 2 * couples:2], tallies[2:2 + 2 * couples:2]
    margin = jnp.minimum(giver - 1, limit - receiver)
    passed = jax.random.randint(jax.random.fold_in(stream_key, 1), (couples,), 0, 1 << 20) % (margin + 1)
    tallies = tallies.at[1:1 + 2 * couples:2].set(giver - passed).at[2:2 + 2 * couples:2].set(receiver + passed)
    return tallies[jax.random.permutation(jax.random.fold_in(stream_key, 2), count)]


def normal_values(own_key, shape, deviation, most, cuts=(), held_as=jnp.bfloat16):
    factor_of = block_levels(own_key, shape, cuts, -0.22, 0.18) if cuts else 1.0
    array = jax.random.normal(own_key, shape, jnp.float32) * deviation * factor_of
    return jnp.minimum(jnp.maximum(array, -most), most).astype(held_as)


def setup_inputs(seed: int = 0) -> dict:
    keys = jax.random.split(jax.random.key(seed), 21)
    tokens = normal_values(keys[0], (TOKENS, D), 1.0, 6.0, ((0, 32),))
    lengths = ragged(keys[1], PROMPTS, TOKENS, LONGEST, 2).astype(jnp.int32)
    in_gain = jnp.clip(1.0 + 0.1 * jax.random.normal(keys[2], (D,), jnp.float32), 0.5, 1.5)
    w_query = normal_values(keys[3], (D, HEADS * DK), D ** -0.5, 0.125)
    w_key = draw_w_key(jax.random.fold_in(keys[20], 71), 0)
    w_value = normal_values(keys[5], (D, HEADS * DV), D ** -0.5, 0.125)
    w_gate = normal_values(keys[6], (D, HEADS * DV), D ** -0.5, 0.125)
    w_beta = normal_values(keys[7], (D, HEADS), D ** -0.5, 0.125)
    w_decay = normal_values(keys[8], (D, HEADS), D ** -0.5, 0.125)
    decay_log = draw_decay_log(jax.random.fold_in(keys[20], 71), 0)
    decay_bias = draw_decay_bias(jax.random.fold_in(keys[20], 71), 0)
    conv_query = normal_values(keys[11], (CONV, HEADS * DK), 0.5, 2.5, (), jnp.float32)
    conv_key = normal_values(keys[12], (CONV, HEADS * DK), 0.5, 2.5, (), jnp.float32)
    conv_value = normal_values(keys[13], (CONV, HEADS * DV), 0.5, 2.5, (), jnp.float32)
    head_gain = jnp.clip(1.0 + 0.1 * jax.random.normal(keys[14], (DV,), jnp.float32), 0.5, 1.5)
    w_out = normal_values(keys[15], (HEADS * DV, D), (HEADS * DV) ** -0.5, 0.09375)
    mlp_gain = jnp.clip(1.0 + 0.1 * jax.random.normal(keys[16], (D,), jnp.float32), 0.5, 1.5)
    w_up_gate = normal_values(keys[17], (D, FF), D ** -0.5, 0.125, ((0, 32),))
    w_up = normal_values(keys[18], (D, FF), D ** -0.5, 0.125, ((0, 32),))
    w_down = normal_values(keys[19], (FF, D), FF ** -0.5, 0.078125, ((1, 32),))
    return {"tokens": tokens, "lengths": lengths, "in_gain": in_gain, "w_query": w_query, "w_key": w_key, "w_value": w_value, "w_gate": w_gate, "w_beta": w_beta, "w_decay": w_decay, "decay_log": decay_log, "decay_bias": decay_bias, "conv_query": conv_query, "conv_key": conv_key, "conv_value": conv_value, "head_gain": head_gain, "w_out": w_out, "mlp_gain": mlp_gain, "w_up_gate": w_up_gate, "w_up": w_up, "w_down": w_down}


maximal_matmul_accuracy = lax.Precision.HIGHEST

def rms_scale(values, gain):
    mean_square = lax.optimization_barrier(jnp.mean(values * values, axis=-1, keepdims=True))
    return values / jnp.sqrt(mean_square + 1e-06) * gain

def unit_norm(values):
    return values / jnp.sqrt(lax.optimization_barrier(jnp.sum(values * values, axis=-1, keepdims=True)) + 1e-06)

def segment_of(positions, lengths):
    bounds = jnp.cumsum(lengths).astype(jnp.int32)[:-1]
    return lax.optimization_barrier(jnp.sum((positions[:, None] >= bounds[None, :]).astype(jnp.int32), axis=1)).astype(jnp.int32)

def causal_conv(projected, rim_rows, kernel, segment_ids, rim_segments):
    taps_count = kernel.shape[0]
    row_count = projected.shape[0]
    extended = jnp.concatenate([rim_rows, projected], axis=0).astype(jnp.float32)
    extended_ids = jnp.concatenate([rim_segments, segment_ids], axis=0)
    accumulated = jnp.zeros(projected.shape, jnp.float32)
    for offset in range(taps_count):
        window = lax.slice_in_dim(extended, offset, offset + row_count, axis=0)
        window_ids = lax.slice_in_dim(extended_ids, offset, offset + row_count, axis=0)
        same_doc = (window_ids == segment_ids)[:, None]
        accumulated = accumulated + kernel[offset][None, :] * jnp.where(same_doc, window, 0.0)
    return accumulated

def group_parts(query_vecs, key_vecs, value_vecs, beta_vals, log_decay, segment_ids, prior_segment):
    group_rows = query_vecs.shape[0]
    value_dim = value_vecs.shape[-1]
    cumulative = jnp.cumsum(log_decay, axis=0)
    row_index = jnp.arange(group_rows)[:, None]
    col_index = jnp.arange(group_rows)[None, :]
    same_doc = segment_ids[:, None] == segment_ids[None, :]
    keep_mask = ((row_index >= col_index) & same_doc)[None, :, :]
    strict_mask = (row_index > col_index)[None, :, :]
    head_cumul = jnp.transpose(cumulative)
    gaps = head_cumul[:, :, None] - head_cumul[:, None, :]
    weights = jnp.where(keep_mask, jnp.exp(jnp.where(keep_mask, gaps, 0.0)), 0.0)
    open_mask = (segment_ids == prior_segment).astype(query_vecs.dtype)
    start_decay = jnp.exp(cumulative) * open_mask[:, None]
    key_dots = jnp.einsum('ihd,jhd->hij', key_vecs, key_vecs, precision=maximal_matmul_accuracy)
    coupling = jnp.where(strict_mask, jnp.transpose(beta_vals)[:, :, None] * weights * key_dots, 0.0)
    system = coupling + jnp.eye(group_rows, dtype=query_vecs.dtype)[None]
    targets = jnp.concatenate([beta_vals[:, :, None] * value_vecs, (beta_vals * start_decay)[:, :, None] * key_vecs], axis=-1)
    solved = jax.scipy.linalg.solve_triangular(system, jnp.transpose(targets, (1, 0, 2)), lower=True, unit_diagonal=True)
    starting_value_rows = solved[:, :, :value_dim]
    delta_correction = solved[:, :, value_dim:]
    query_dots = weights * jnp.einsum('ihd,jhd->hij', query_vecs, key_vecs, precision=maximal_matmul_accuracy)
    query_begin_offset = query_vecs * start_decay[:, :, None]
    final_key_rows = key_vecs * jnp.transpose(weights[:, -1, :])[:, :, None]
    carried_decay_factor = start_decay[-1]
    return (starting_value_rows, delta_correction, query_dots, query_begin_offset, final_key_rows, carried_decay_factor)

def group_step(running_state, parts):
    starting_value_rows, delta_correction, query_dots, query_begin_offset, final_key_rows, carried_decay_factor = parts
    fresh_state_update = starting_value_rows - jnp.einsum('mxf,mft->mxt', delta_correction, running_state, precision=maximal_matmul_accuracy)
    output_rows = jnp.einsum('fob,obt->fot', query_begin_offset, running_state, precision=maximal_matmul_accuracy)
    output_rows = output_rows + jnp.einsum('hij,hjv->ihv', query_dots, fresh_state_update, precision=maximal_matmul_accuracy)
    updated_state = carried_decay_factor[:, None, None] * running_state + jnp.einsum('new,enr->ewr', final_key_rows, fresh_state_update, precision=maximal_matmul_accuracy)
    return (updated_state, output_rows)

def reference(tokens, lengths, in_gain, w_query, w_key, w_value, w_gate, w_beta, w_decay, decay_log, decay_bias, conv_query, conv_key, conv_value, head_gain, w_out, mlp_gain, w_up_gate, w_up, w_down):
    token_rows = tokens.astype(jnp.float32)
    normed = rms_scale(token_rows, in_gain).astype(jnp.bfloat16)
    positions = jnp.arange(TOKENS, dtype=jnp.int32)
    segment_ids = segment_of(positions, lengths)
    taps_count = conv_query.shape[0]
    rim_segments = segment_of(jnp.arange(taps_count - 1, dtype=jnp.int32) - (taps_count - 1), lengths)

    def convolved(weight, kernel):
        projected = jnp.dot(normed.astype(jnp.float32), weight.astype(jnp.float32), preferred_element_type=jnp.float32).astype(jnp.bfloat16)
        rim_rows = jnp.zeros((taps_count - 1, projected.shape[1]), jnp.bfloat16)
        return jax.nn.silu(causal_conv(projected, rim_rows, kernel, segment_ids, rim_segments))
    query_vecs = unit_norm(convolved(w_query, conv_query).reshape(TOKENS, HEADS, DK)) * DK ** (-0.5)
    key_vecs = unit_norm(convolved(w_key, conv_key).reshape(TOKENS, HEADS, DK))
    value_vecs = convolved(w_value, conv_value).reshape(TOKENS, HEADS, DV)
    gate_lin = jnp.dot(normed.astype(jnp.float32), w_gate.astype(jnp.float32), preferred_element_type=jnp.float32).astype(jnp.bfloat16)
    beta_vals = jax.nn.sigmoid(jnp.dot(normed.astype(jnp.float32), w_beta.astype(jnp.float32), preferred_element_type=jnp.float32))
    log_decay = -jnp.exp(decay_log) * jax.nn.softplus(jnp.dot(normed.astype(jnp.float32), w_decay.astype(jnp.float32), preferred_element_type=jnp.float32) + decay_bias)
    group_total = TOKENS // GROUP

    def shaped(values):
        return values.reshape((group_total, GROUP) + values.shape[1:])
    prior_ids = segment_of(jnp.arange(group_total, dtype=jnp.int32) * GROUP - 1, lengths)

    def advance(running_state, inputs_one):
        return group_step(running_state, group_parts(*inputs_one))
    initial = jnp.zeros((HEADS, DK, DV), jnp.float32)
    _, output_rows = lax.scan(advance, initial, (shaped(query_vecs), shaped(key_vecs), shaped(value_vecs), shaped(beta_vals), shaped(log_decay), shaped(segment_ids), prior_ids))
    output_rows = output_rows.reshape(TOKENS, HEADS, DV)
    gate_vals = jax.nn.silu(gate_lin.astype(jnp.float32)).reshape(TOKENS, HEADS, DV)
    head_out = (rms_scale(output_rows, head_gain) * gate_vals).reshape(TOKENS, HEADS * DV).astype(jnp.bfloat16)
    resid = token_rows + jnp.dot(head_out.astype(jnp.float32), w_out.astype(jnp.float32), preferred_element_type=jnp.float32)
    mlp_in = rms_scale(resid, mlp_gain).astype(jnp.bfloat16)
    gate_acc = jnp.dot(mlp_in.astype(jnp.float32), w_up_gate.astype(jnp.float32), preferred_element_type=jnp.float32)
    up_acc = jnp.dot(mlp_in.astype(jnp.float32), w_up.astype(jnp.float32), preferred_element_type=jnp.float32)
    hidden = (jax.nn.silu(gate_acc) * up_acc).astype(jnp.bfloat16)
    return (resid + jnp.dot(hidden.astype(jnp.float32), w_down.astype(jnp.float32), preferred_element_type=jnp.float32)).astype(jnp.bfloat16)
```

```python
import functools
import jax
import jax.numpy as jnp
from jax import lax
from jax.experimental import pallas as pl
from jax.experimental.pallas import tpu as pltpu
from jax.sharding import PartitionSpec as P

RIM = 16
F32 = jnp.float32
BF16 = jnp.bfloat16


def rms_scale(values, gain):
    mean_square = jnp.mean(values * values, axis=-1, keepdims=True)
    return values / jnp.sqrt(mean_square + 1e-06) * gain


def segment_of(positions, lengths):
    bounds = jnp.cumsum(lengths)[:-1]
    return jnp.sum((positions[:, None] >= bounds[None, :]).astype(jnp.int32), axis=1)


def mm(a, b):
    return jnp.dot(a, b, preferred_element_type=F32)


def mm_t(a, b):
    return lax.dot_general(a, b, (((1,), (1,)), ((), ())), preferred_element_type=F32)


def split(a):
    high = a.astype(BF16)
    return high, (a - high.astype(F32)).astype(BF16)


def mm3(a, b):
    ah, al = a
    bh, bl = b
    return mm(ah, bh) + (mm(ah, bl) + mm(al, bh))


def conv_silu(p_ref, taps_ref, lanes, scratch, masks, rows):
    scratch[...] = p_ref[:, lanes].astype(F32)
    taps = taps_ref.shape[0]
    acc = None
    for i in range(taps):
        back = taps - 1 - i
        window = scratch[pl.ds(RIM - back, rows), :]
        term = taps_ref[i : i + 1, lanes] * window
        if back:
            term = term * masks[back - 1]
        acc = term if acc is None else acc + term
    return acc / (1.0 + jnp.exp(-acc))


def local_kernel(
    chunk, dk, dv, pq, pk, pv, tq, tk, tv, scal, qeff, oloc, maps, scr_q, scr_k, scr_v
):
    heads = scal.shape[0]
    rows = scal.shape[2]
    count = rows // chunk
    row_i = lax.broadcasted_iota(jnp.int32, (chunk, chunk), 0)
    col_i = lax.broadcasted_iota(jnp.int32, (chunk, chunk), 1)
    eye = (row_i == col_i).astype(F32)
    pairs = [(h, c) for h in range(heads) for c in range(count)]
    cols, lanes, keys, queries, values = [], [], [], [], []
    for h in range(heads):
        lane = scal[h]
        col = lane.T
        masks = [col[:, 6 + s : 7 + s] for s in range(3)]
        q = conv_silu(pq, tq, slice(h * dk, (h + 1) * dk), scr_q.at[h], masks, rows)
        k = conv_silu(pk, tk, slice(h * dk, (h + 1) * dk), scr_k.at[h], masks, rows)
        v = conv_silu(pv, tv, slice(h * dv, (h + 1) * dv), scr_v.at[h], masks, rows)
        q = q * (lax.rsqrt(jnp.sum(q * q, axis=-1, keepdims=True) + 1e-06) * dk ** (-0.5))
        k = k * lax.rsqrt(jnp.sum(k * k, axis=-1, keepdims=True) + 1e-06)
        cols.append(col)
        lanes.append(lane)
        queries.append(q.astype(BF16))
        keys.append(k.astype(BF16))
        values.append(v * col[:, 0:1])
    lower, attend, inverse = {}, {}, {}
    for h, c in pairs:
        part = slice(c * chunk, (c + 1) * chunk)
        col, lane = cols[h][part], lanes[h][:, part]
        kb, qb = keys[h][part], queries[h][part]
        keep = (row_i >= col_i) & (col[:, 5:6] == lane[5:6, :])
        gaps = col[:, 1:2] - lane[1:2, :]
        weights = jnp.where(keep, jnp.exp(jnp.where(keep, gaps, 0.0)), 0.0)
        dots = mm_t(jnp.concatenate([kb, qb], axis=0), kb)
        lower[h, c] = jnp.where(row_i > col_i, col[:, 0:1] * weights * dots[:chunk], 0.0)
        attend[h, c] = (weights * dots[chunk:]).astype(BF16)
    shift = 0
    while (1 << shift) < chunk:
        level = ((row_i >> shift) != (col_i >> shift)) & (
            (row_i >> (shift + 1)) == (col_i >> (shift + 1))
        )
        if shift == 0:
            for p in pairs:
                inverse[p] = eye - jnp.where(level, lower[p], 0.0)
        else:
            halves = {p: split(inverse[p]) for p in pairs}
            mid = {p: mm3(halves[p], split(jnp.where(level, lower[p], 0.0))) for p in pairs}
            for p in pairs:
                inverse[p] = inverse[p] - mm3(split(mid[p]), halves[p])
        shift += 1
    start = jnp.concatenate(
        [
            (
                lax.broadcasted_iota(jnp.int32, (dk, dk), 0)
                == lax.broadcasted_iota(jnp.int32, (dk, dk), 1)
            ).astype(F32),
            jnp.zeros((dk, dv), F32),
        ],
        axis=1,
    )
    state = [start for _ in range(heads)]
    for c in range(count):
        part = slice(c * chunk, (c + 1) * chunk)
        for h in range(heads):
            col, lane = cols[h][part], lanes[h][:, part]
            kb, qb = keys[h][part], queries[h][part]
            sd = col[:, 2:3]
            both = mm(jnp.concatenate([kb, qb], axis=0), state[h].astype(BF16))
            fresh = jnp.concatenate(
                [jnp.zeros((chunk, dk), F32), values[h][part]], axis=1
            ) - (col[:, 0:1] * sd) * both[:chunk]
            update = mm(inverse[h, c].astype(BF16), fresh.astype(BF16))
            out = sd * both[chunk:] + mm(attend[h, c], update.astype(BF16))
            qeff[h, part, :] = out[:, :dk].astype(BF16)
            oloc[h, part, :] = out[:, dk:].astype(BF16)
            final = (col[:, 3:4] * update).astype(BF16)
            state[h] = lane[4:5, 0:1] * state[h] + mm(kb.astype(F32).T.astype(BF16), final)
    for h in range(heads):
        maps[h] = state[h].astype(BF16)


def local_maps(pq, pk, pv, tq, tk, tv, scal, chunk, per_step):
    heads, extra, rows = scal.shape
    dk, dv = pq.shape[1] // heads, pv.shape[1] // heads
    ext = pq.shape[0]
    by_lane = lambda r, w: pl.BlockSpec((r, w * per_step), lambda g: (0, g))
    by_head = lambda r, w: pl.BlockSpec((per_step, r, w), lambda g: (g, 0, 0))
    taps = tq.shape[0]
    return pl.pallas_call(
        functools.partial(local_kernel, chunk, dk, dv),
        grid=(heads // per_step,),
        in_specs=[
            by_lane(ext, dk),
            by_lane(ext, dk),
            by_lane(ext, dv),
            by_lane(taps, dk),
            by_lane(taps, dk),
            by_lane(taps, dv),
            by_head(extra, rows),
        ],
        out_specs=[by_head(rows, dk), by_head(rows, dv), by_head(dk, dk + dv)],
        out_shape=[
            jax.ShapeDtypeStruct((heads, rows, dk), BF16),
            jax.ShapeDtypeStruct((heads, rows, dv), BF16),
            jax.ShapeDtypeStruct((heads, dk, dk + dv), BF16),
        ],
        scratch_shapes=[
            pltpu.VMEM((per_step, ext, dk), F32),
            pltpu.VMEM((per_step, ext, dk), F32),
            pltpu.VMEM((per_step, ext, dv), F32),
        ],
        compiler_params=pltpu.CompilerParams(vmem_limit_bytes=48 * 2**20),
        cost_estimate=pl.CostEstimate(
            flops=heads * rows * 2000000, bytes_accessed=20 * 2**20, transcendentals=0
        ),
        name="local_maps",
    )(pq, pk, pv, tq, tk, tv, scal)


def chain_kernel(n, dk, maps, states, landing, outgoing, send_sem, recv_sem):
    me = lax.axis_index("req")
    heads = maps.shape[0]
    barrier = pltpu.get_barrier_semaphore()
    has_left, has_right = me > 0, me < n - 1

    @pl.when(has_left)
    def _():
        pl.semaphore_signal(
            barrier, inc=1, device_id={"req": me - 1}, device_id_type=pl.DeviceIdType.MESH
        )

    @pl.when(has_right)
    def _():
        pl.semaphore_wait(barrier, 1)

    def copy(h):
        return pltpu.make_async_remote_copy(
            src_ref=outgoing.at[h],
            dst_ref=landing.at[h],
            send_sem=send_sem.at[h],
            recv_sem=recv_sem.at[h],
            device_id={"req": me + 1},
            device_id_type=pl.DeviceIdType.MESH,
        )

    def one(h, carry):
        @pl.when(has_left)
        def _():
            copy(h).wait_recv()
            coming = landing[h]
            states[h] = coming
            onward = mm(maps[h, :, :dk], coming) + maps[h, :, dk:].astype(F32)
            outgoing[h] = onward.astype(BF16)

        @pl.when(me == 0)
        def _():
            states[h] = jnp.zeros(states.shape[1:], BF16)
            outgoing[h] = maps[h, :, dk:]

        @pl.when(has_right)
        def _():
            copy(h).start()

        return carry

    lax.fori_loop(0, heads, one, 0)

    def drain(h, carry):
        copy(h).wait_send()
        return carry

    @pl.when(has_right)
    def _():
        lax.fori_loop(0, heads, drain, 0)


def chain_states(maps, n):
    heads, dk, width = maps.shape
    dv = width - dk
    return pl.pallas_call(
        functools.partial(chain_kernel, n, dk),
        in_specs=[pl.BlockSpec(memory_space=pltpu.VMEM)],
        out_specs=pl.BlockSpec(memory_space=pltpu.VMEM),
        out_shape=jax.ShapeDtypeStruct((heads, dk, dv), BF16),
        scratch_shapes=[
            pltpu.VMEM((heads, dk, dv), BF16),
            pltpu.VMEM((heads, dk, dv), BF16),
            pltpu.SemaphoreType.DMA((heads,)),
            pltpu.SemaphoreType.DMA((heads,)),
        ],
        compiler_params=pltpu.CompilerParams(
            collective_id=0, has_side_effects=True, vmem_limit_bytes=32 * 2**20
        ),
        cost_estimate=pl.CostEstimate(
            flops=60 * 10**9, bytes_accessed=3 * 2**20, transcendentals=0
        ),
        name="chain_states",
    )(maps)


def finish_kernel(qeff, oloc, states, gate, gain, out):
    heads, dv = oloc.shape[0], oloc.shape[2]
    for h in range(heads):
        lanes = slice(h * dv, (h + 1) * dv)
        rec = mm(qeff[h], states[h]) + oloc[h].astype(F32)
        rec = rec * lax.rsqrt(jnp.mean(rec * rec, axis=-1, keepdims=True) + 1e-06)
        g = gate[:, lanes].astype(F32)
        out[:, lanes] = (rec * gain[...] * (g / (1.0 + jnp.exp(-g)))).astype(BF16)


def finish_heads(qeff, oloc, states, gate, gain, per_step):
    heads, rows, dk = qeff.shape
    dv = oloc.shape[2]
    by_head = lambda r, w: pl.BlockSpec((per_step, r, w), lambda g: (g, 0, 0))
    lane = pl.BlockSpec((rows, dv * per_step), lambda g: (0, g))
    return pl.pallas_call(
        finish_kernel,
        grid=(heads // per_step,),
        in_specs=[
            by_head(rows, dk),
            by_head(rows, dv),
            by_head(dk, dv),
            lane,
            pl.BlockSpec((1, dv), lambda g: (0, 0)),
        ],
        out_specs=lane,
        out_shape=jax.ShapeDtypeStruct((rows, heads * dv), BF16),
        compiler_params=pltpu.CompilerParams(vmem_limit_bytes=32 * 2**20),
        cost_estimate=pl.CostEstimate(
            flops=2 * heads * rows * dk * dv, bytes_accessed=12 * 2**20, transcendentals=0
        ),
        name="finish_heads",
    )(qeff, oloc, states, gate, gain.reshape(1, dv))


def swap_cores(value, n):
    return lax.ppermute(value, "req", [(i, i ^ 1) for i in range(n)])


def per_device(
    tokens,
    lengths,
    in_gain,
    w_query,
    w_key,
    w_value,
    w_gate,
    w_beta,
    w_decay,
    decay_log,
    decay_bias,
    conv_query,
    conv_key,
    conv_value,
    head_gain,
    w_out,
    mlp_gain,
    w_up_gate,
    w_up,
    w_down,
):
    n = lax.axis_size("req")
    me = lax.axis_index("req")
    core = me % 2
    share_rows = tokens.shape[0]
    gathered = lax.all_gather(tokens, "mlp", axis=0, tiled=True)
    rows = gathered.shape[0]
    heads = w_beta.shape[1]
    taps = conv_query.shape[0]
    chunk = 128
    count = rows // chunk
    half = w_up.shape[1] // 2

    def weight_half(shard):
        mine = lax.dynamic_slice_in_dim(shard, core * half, half, 1)
        other = lax.dynamic_slice_in_dim(shard, (1 - core) * half, half, 1)
        theirs = swap_cores(other, n)
        first = jnp.where(core == 0, mine, theirs)
        second = jnp.where(core == 0, theirs, mine)
        both = jnp.concatenate([first, second], axis=0)
        groups = [list(range(0, n, 2)), list(range(1, n, 2))]
        return lax.all_gather(both, "req", axis=0, tiled=True, axis_index_groups=groups)

    up_gate_half = weight_half(w_up_gate)
    up_half = weight_half(w_up)
    down_half = weight_half(w_down.T)

    rim = lax.ppermute(gathered[rows - RIM :], "req", [(i, i + 1) for i in range(n - 1)])
    token_rows = gathered.astype(F32)
    normed = rms_scale(token_rows, in_gain).astype(BF16)
    gate_lin = mm(normed, w_gate).astype(BF16)
    small = mm(normed, jnp.concatenate([w_beta, w_decay], axis=1))
    rim_normed = rms_scale(rim.astype(F32), in_gain).astype(BF16)
    ext = jnp.concatenate([rim_normed, normed], axis=0)
    pq = mm(ext, w_query).astype(BF16)
    pk = mm(ext, w_key).astype(BF16)
    pv = mm(ext, w_value).astype(BF16)

    beta = jax.nn.sigmoid(small[:, :heads]).T
    gdec = (-jnp.exp(decay_log) * jax.nn.softplus(small[:, heads:] + decay_bias)).T
    piece_start = me * rows
    reach = piece_start - (taps - 1) + jnp.arange(rows + taps - 1, dtype=jnp.int32)
    seg_all = segment_of(reach, lengths)
    seg = seg_all[taps - 1 :]
    seg_chunks = seg.reshape(count, chunk)
    prior = segment_of(
        piece_start + jnp.arange(count, dtype=jnp.int32) * chunk - 1, lengths
    )
    opened = (seg_chunks == prior[:, None]).astype(F32)
    to_last = (seg_chunks == seg_chunks[:, -1:]).astype(F32)
    upper = jnp.triu(jnp.ones((chunk, chunk), F32))
    cum = jnp.dot(
        gdec.reshape(heads * count, chunk), upper, precision=lax.Precision.HIGHEST
    ).reshape(heads, count, chunk)
    start_decay = jnp.exp(cum) * opened[None]
    final_w = jnp.exp(cum[:, :, -1:] - cum) * to_last[None]
    carry = jnp.broadcast_to(start_decay[:, :, -1:], cum.shape)

    def flat(a):
        return a.reshape(heads, 1, rows)

    def shared(a):
        return jnp.broadcast_to(a.astype(F32).reshape(1, 1, rows), (heads, 1, rows))

    masks = [
        shared(seg_all[taps - 1 - s : taps - 1 - s + rows] == seg) for s in range(1, taps)
    ]
    scal = jnp.concatenate(
        [flat(beta), flat(cum), flat(start_decay), flat(final_w), flat(carry), shared(seg)]
        + masks
        + [jnp.zeros((heads, 16 - 6 - len(masks), rows), F32)],
        axis=1,
    )
    qeff, oloc, maps = local_maps(
        pq, pk, pv, conv_query, conv_key, conv_value, scal, chunk, 2
    )
    states = chain_states(maps, n)
    head_out = finish_heads(qeff, oloc, states, gate_lin, head_gain, 2)
    partial_out = mm(head_out, w_out)
    if lax.axis_size("mlp") > 1:
        partial_out = lax.psum(partial_out.astype(BF16), "mlp").astype(F32)
    resid = token_rows + partial_out
    mlp_in = rms_scale(resid, mlp_gain).astype(BF16)
    pair_in = jnp.concatenate([mlp_in, swap_cores(mlp_in, n)], axis=0)
    hidden = (jax.nn.silu(mm(pair_in, up_gate_half)) * mm(pair_in, up_half)).astype(BF16)
    down_theirs = mm_t(hidden[rows:], down_half).astype(BF16)
    from_partner = swap_cores(down_theirs, n).astype(F32)
    down = mm_t(hidden[:rows], down_half) + from_partner
    if lax.axis_size("mlp") > 1:
        down = lax.psum_scatter(
            down.astype(BF16), "mlp", scatter_dimension=0, tiled=True
        ).astype(F32)
        resid = lax.dynamic_slice_in_dim(
            resid, lax.axis_index("mlp") * share_rows, share_rows, 0
        )
    return (resid + down).astype(BF16)


def solution(mesh):
    placed = (
        P(("req", "mlp"), None),
        P(),
        P(),
        P(None, "mlp"),
        P(None, "mlp"),
        P(None, "mlp"),
        P(None, "mlp"),
        P(None, "mlp"),
        P(None, "mlp"),
        P("mlp"),
        P("mlp"),
        P(None, "mlp"),
        P(None, "mlp"),
        P(None, "mlp"),
        P(),
        P("mlp", None),
        P(),
        P("req", "mlp"),
        P("req", "mlp"),
        P("mlp", "req"),
    )
    return jax.shard_map(
        per_device, mesh=mesh, in_specs=placed, out_specs=P(("req", "mlp"), None), check_vma=False
    )
```

```python
import functools
import jax
import jax.numpy as jnp
from jax import lax
from jax.experimental import pallas as pl
from jax.experimental.pallas import tpu as pltpu
from jax.sharding import PartitionSpec as P

RIM = 16
F32 = jnp.float32
BF16 = jnp.bfloat16


def rms_scale(values, gain):
    mean_square = jnp.mean(values * values, axis=-1, keepdims=True)
    return values / jnp.sqrt(mean_square + 1e-06) * gain


def segment_of(positions, lengths):
    bounds = jnp.cumsum(lengths)[:-1]
    return jnp.sum((positions[:, None] >= bounds[None, :]).astype(jnp.int32), axis=1)


def mm(a, b):
    return jnp.dot(a, b, preferred_element_type=F32)


def mm_t(a, b):
    return lax.dot_general(a, b, (((1,), (1,)), ((), ())), preferred_element_type=F32)


def split(a):
    high = a.astype(BF16)
    return high, (a - high.astype(F32)).astype(BF16)


def mm3(a, b):
    ah, al = a
    bh, bl = b
    return mm(ah, bh) + (mm(ah, bl) + mm(al, bh))


def conv_silu(p_ref, taps_ref, lanes, scratch, masks, rows):
    scratch[...] = p_ref[:, lanes].astype(F32)
    taps = taps_ref.shape[0]
    acc = None
    for i in range(taps):
        back = taps - 1 - i
        window = scratch[pl.ds(RIM - back, rows), :]
        term = taps_ref[i : i + 1, lanes] * window
        if back:
            term = term * masks[back - 1]
        acc = term if acc is None else acc + term
    return acc / (1.0 + jnp.exp(-acc))


def local_kernel(
    chunk, dk, dv, pq, pk, pv, tq, tk, tv, scal, qeff, oloc, maps, scr_q, scr_k, scr_v
):
    heads = scal.shape[0]
    rows = scal.shape[2]
    count = rows // chunk
    row_i = lax.broadcasted_iota(jnp.int32, (chunk, chunk), 0)
    col_i = lax.broadcasted_iota(jnp.int32, (chunk, chunk), 1)
    eye = (row_i == col_i).astype(F32)
    pairs = [(h, c) for h in range(heads) for c in range(count)]
    cols, lanes, keys, queries, values = [], [], [], [], []
    for h in range(heads):
        lane = scal[h]
        col = lane.T
        masks = [col[:, 6 + s : 7 + s] for s in range(3)]
        q = conv_silu(pq, tq, slice(h * dk, (h + 1) * dk), scr_q.at[h], masks, rows)
        k = conv_silu(pk, tk, slice(h * dk, (h + 1) * dk), scr_k.at[h], masks, rows)
        v = conv_silu(pv, tv, slice(h * dv, (h + 1) * dv), scr_v.at[h], masks, rows)
        q = q * (lax.rsqrt(jnp.sum(q * q, axis=-1, keepdims=True) + 1e-06) * dk ** (-0.5))
        k = k * lax.rsqrt(jnp.sum(k * k, axis=-1, keepdims=True) + 1e-06)
        cols.append(col)
        lanes.append(lane)
        queries.append(q.astype(BF16))
        keys.append(k.astype(BF16))
        values.append(v * col[:, 0:1])
    lower, attend, inverse = {}, {}, {}
    for h, c in pairs:
        part = slice(c * chunk, (c + 1) * chunk)
        col, lane = cols[h][part], lanes[h][:, part]
        kb, qb = keys[h][part], queries[h][part]
        keep = (row_i >= col_i) & (col[:, 5:6] == lane[5:6, :])
        gaps = col[:, 1:2] - lane[1:2, :]
        weights = jnp.where(keep, jnp.exp(jnp.where(keep, gaps, 0.0)), 0.0)
        dots = mm_t(jnp.concatenate([kb, qb], axis=0), kb)
        lower[h, c] = jnp.where(row_i > col_i, col[:, 0:1] * weights * dots[:chunk], 0.0)
        attend[h, c] = (weights * dots[chunk:]).astype(BF16)
    shift = 0
    while (1 << shift) < chunk:
        level = ((row_i >> shift) != (col_i >> shift)) & (
            (row_i >> (shift + 1)) == (col_i >> (shift + 1))
        )
        if shift == 0:
            for p in pairs:
                inverse[p] = eye - jnp.where(level, lower[p], 0.0)
        else:
            halves = {p: split(inverse[p]) for p in pairs}
            mid = {p: mm3(halves[p], split(jnp.where(level, lower[p], 0.0))) for p in pairs}
            for p in pairs:
                inverse[p] = inverse[p] - mm3(split(mid[p]), halves[p])
        shift += 1
    start = jnp.concatenate(
        [
            (
                lax.broadcasted_iota(jnp.int32, (dk, dk), 0)
                == lax.broadcasted_iota(jnp.int32, (dk, dk), 1)
            ).astype(F32),
            jnp.zeros((dk, dv), F32),
        ],
        axis=1,
    )
    state = [start for _ in range(heads)]
    for c in range(count):
        part = slice(c * chunk, (c + 1) * chunk)
        for h in range(heads):
            col, lane = cols[h][part], lanes[h][:, part]
            kb, qb = keys[h][part], queries[h][part]
            sd = col[:, 2:3]
            both = mm(jnp.concatenate([kb, qb], axis=0), state[h].astype(BF16))
            fresh = jnp.concatenate(
                [jnp.zeros((chunk, dk), F32), values[h][part]], axis=1
            ) - (col[:, 0:1] * sd) * both[:chunk]
            update = mm(inverse[h, c].astype(BF16), fresh.astype(BF16))
            out = sd * both[chunk:] + mm(attend[h, c], update.astype(BF16))
            qeff[h, part, :] = out[:, :dk].astype(BF16)
            oloc[h, part, :] = out[:, dk:].astype(BF16)
            final = (col[:, 3:4] * update).astype(BF16)
            state[h] = lane[4:5, 0:1] * state[h] + mm(kb.astype(F32).T.astype(BF16), final)
    for h in range(heads):
        maps[h] = state[h].astype(BF16)


def local_maps(pq, pk, pv, tq, tk, tv, scal, chunk, per_step):
    heads, extra, rows = scal.shape
    dk, dv = pq.shape[1] // heads, pv.shape[1] // heads
    ext = pq.shape[0]
    by_lane = lambda r, w: pl.BlockSpec((r, w * per_step), lambda g: (0, g))
    by_head = lambda r, w: pl.BlockSpec((per_step, r, w), lambda g: (g, 0, 0))
    taps = tq.shape[0]
    return pl.pallas_call(
        functools.partial(local_kernel, chunk, dk, dv),
        grid=(heads // per_step,),
        in_specs=[
            by_lane(ext, dk),
            by_lane(ext, dk),
            by_lane(ext, dv),
            by_lane(taps, dk),
            by_lane(taps, dk),
            by_lane(taps, dv),
            by_head(extra, rows),
        ],
        out_specs=[by_head(rows, dk), by_head(rows, dv), by_head(dk, dk + dv)],
        out_shape=[
            jax.ShapeDtypeStruct((heads, rows, dk), BF16),
            jax.ShapeDtypeStruct((heads, rows, dv), BF16),
            jax.ShapeDtypeStruct((heads, dk, dk + dv), BF16),
        ],
        scratch_shapes=[
            pltpu.VMEM((per_step, ext, dk), F32),
            pltpu.VMEM((per_step, ext, dk), F32),
            pltpu.VMEM((per_step, ext, dv), F32),
        ],
        compiler_params=pltpu.CompilerParams(vmem_limit_bytes=48 * 2**20),
        cost_estimate=pl.CostEstimate(
            flops=heads * rows * 2000000, bytes_accessed=20 * 2**20, transcendentals=0
        ),
        name="local_maps",
    )(pq, pk, pv, tq, tk, tv, scal)


def chain_kernel(
    n, dk, maps, states, theirs, first, joined, landing, outgoing, to_peer, from_peer,
    swap_send, swap_recv, send_sem, recv_sem, peer_send, peer_recv
):
    me = lax.axis_index("req")
    core = lax.rem(me, 2)
    peer = me + 1 - 2 * core
    per_core = joined.shape[0]
    has_left, has_right = me >= 2, me < n - 2
    barrier = pltpu.get_barrier_semaphore()
    mesh_id = pl.DeviceIdType.MESH
    pl.semaphore_signal(barrier, inc=1, device_id={"req": peer}, device_id_type=mesh_id)

    @pl.when(has_left)
    def _():
        pl.semaphore_signal(barrier, inc=1, device_id={"req": me - 2}, device_id_type=mesh_id)

    pl.semaphore_wait(barrier, 1 + has_right.astype(jnp.int32))
    own_base = core * per_core
    peer_base = (1 - core) * per_core

    swap = pltpu.make_async_remote_copy(
        src_ref=maps.at[pl.ds(peer_base, per_core)],
        dst_ref=theirs,
        send_sem=swap_send,
        recv_sem=swap_recv,
        device_id={"req": peer},
        device_id_type=mesh_id,
    )
    swap.start()
    swap.wait_recv()

    def join(h, carry):
        mine, other = maps[own_base + h], theirs[h]
        early = jnp.where(core == 0, mine, other)
        late = jnp.where(core == 0, other, mine)
        both = mm(late[:, :dk], early)
        first[h] = early
        joined[h, :, :dk] = both[:, :dk].astype(BF16)
        joined[h, :, dk:] = (both[:, dk:] + late[:, dk:].astype(F32)).astype(BF16)
        return carry

    lax.fori_loop(0, per_core, join, 0)

    def onward_copy(h):
        return pltpu.make_async_remote_copy(
            src_ref=outgoing.at[h],
            dst_ref=landing.at[h],
            send_sem=send_sem.at[h],
            recv_sem=recv_sem.at[h],
            device_id={"req": me + 2},
            device_id_type=mesh_id,
        )

    def peer_copy(h):
        return pltpu.make_async_remote_copy(
            src_ref=to_peer.at[h],
            dst_ref=from_peer.at[h],
            send_sem=peer_send.at[h],
            recv_sem=peer_recv.at[h],
            device_id={"req": peer},
            device_id_type=mesh_id,
        )

    def one(h, carry):
        @pl.when(has_left)
        def _():
            onward_copy(h).wait_recv()

        @pl.when(jnp.logical_not(has_left))
        def _():
            landing[h] = jnp.zeros(landing.shape[1:], BF16)

        coming = landing[h]

        @pl.when(has_right)
        def _():
            onward = mm(joined[h, :, :dk], coming) + joined[h, :, dk:].astype(F32)
            outgoing[h] = onward.astype(BF16)
            onward_copy(h).start()

        middle = (mm(first[h, :, :dk], coming) + first[h, :, dk:].astype(F32)).astype(BF16)
        states[own_base + h] = jnp.where(core == 0, coming, middle)
        to_peer[h] = jnp.where(core == 0, middle, coming)
        peer_copy(h).start()
        return carry

    lax.fori_loop(0, per_core, one, 0)

    def collect(h, carry):
        peer_copy(h).wait_recv()
        states[peer_base + h] = from_peer[h]
        peer_copy(h).wait_send()
        return carry

    lax.fori_loop(0, per_core, collect, 0)

    def drain(h, carry):
        onward_copy(h).wait_send()
        return carry

    @pl.when(has_right)
    def _():
        lax.fori_loop(0, per_core, drain, 0)

    swap.wait_send()


def chain_states(maps, n):
    heads, dk, width = maps.shape
    dv = width - dk
    per_core = heads // 2
    map_buf = pltpu.VMEM((per_core, dk, width), BF16)
    state_buf = pltpu.VMEM((per_core, dk, dv), BF16)
    sems = pltpu.SemaphoreType.DMA((per_core,))
    return pl.pallas_call(
        functools.partial(chain_kernel, n, dk),
        in_specs=[pl.BlockSpec(memory_space=pltpu.VMEM)],
        out_specs=pl.BlockSpec(memory_space=pltpu.VMEM),
        out_shape=jax.ShapeDtypeStruct((heads, dk, dv), BF16),
        scratch_shapes=[map_buf] * 3
        + [state_buf] * 4
        + [pltpu.SemaphoreType.DMA] * 2
        + [sems] * 4,
        compiler_params=pltpu.CompilerParams(
            collective_id=0, has_side_effects=True, vmem_limit_bytes=32 * 2**20
        ),
        cost_estimate=pl.CostEstimate(
            flops=60 * 10**9, bytes_accessed=3 * 2**20, transcendentals=0
        ),
        name="chain_states",
    )(maps)


def finish_kernel(qeff, oloc, states, gate, gain, out):
    heads, dv = oloc.shape[0], oloc.shape[2]
    for h in range(heads):
        lanes = slice(h * dv, (h + 1) * dv)
        rec = mm(qeff[h], states[h]) + oloc[h].astype(F32)
        rec = rec * lax.rsqrt(jnp.mean(rec * rec, axis=-1, keepdims=True) + 1e-06)
        g = gate[:, lanes].astype(F32)
        out[:, lanes] = (rec * gain[...] * (g / (1.0 + jnp.exp(-g)))).astype(BF16)


def finish_heads(qeff, oloc, states, gate, gain, per_step):
    heads, rows, dk = qeff.shape
    dv = oloc.shape[2]
    by_head = lambda r, w: pl.BlockSpec((per_step, r, w), lambda g: (g, 0, 0))
    lane = pl.BlockSpec((rows, dv * per_step), lambda g: (0, g))
    return pl.pallas_call(
        finish_kernel,
        grid=(heads // per_step,),
        in_specs=[
            by_head(rows, dk),
            by_head(rows, dv),
            by_head(dk, dv),
            lane,
            pl.BlockSpec((1, dv), lambda g: (0, 0)),
        ],
        out_specs=lane,
        out_shape=jax.ShapeDtypeStruct((rows, heads * dv), BF16),
        compiler_params=pltpu.CompilerParams(vmem_limit_bytes=32 * 2**20),
        cost_estimate=pl.CostEstimate(
            flops=2 * heads * rows * dk * dv, bytes_accessed=12 * 2**20, transcendentals=0
        ),
        name="finish_heads",
    )(qeff, oloc, states, gate, gain.reshape(1, dv))


def swapped(value, n, bits):
    return lax.ppermute(value, "req", [(i, i ^ bits) for i in range(n)])


def per_device(
    tokens,
    lengths,
    in_gain,
    w_query,
    w_key,
    w_value,
    w_gate,
    w_beta,
    w_decay,
    decay_log,
    decay_bias,
    conv_query,
    conv_key,
    conv_value,
    head_gain,
    w_out,
    mlp_gain,
    w_up_gate,
    w_up,
    w_down,
):
    n = lax.axis_size("req")
    me = lax.axis_index("req")
    share_rows = tokens.shape[0]
    gathered = lax.all_gather(tokens, "mlp", axis=0, tiled=True)
    rows = gathered.shape[0]
    heads = w_beta.shape[1]
    taps = conv_query.shape[0]
    chunk = 128
    count = rows // chunk
    group = 4
    spot = me % group
    quarter = w_up.shape[1] // group
    shards = jnp.concatenate([w_up_gate, w_up, w_down.T], axis=0)
    depth = w_up.shape[0]
    pieces = jnp.zeros((group,) + (shards.shape[0], quarter), BF16)
    for d in range(group):
        piece = lax.dynamic_slice_in_dim(shards, (spot ^ d) * quarter, quarter, 1)
        if d:
            piece = swapped(piece, n, d)
        pieces = lax.dynamic_update_slice_in_dim(pieces, piece[None], spot ^ d, 0)
    members = [list(range(k, n, group)) for k in range(group)]
    up_gate_part, up_part, down_part = [
        lax.all_gather(
            pieces[:, m * depth : (m + 1) * depth].reshape(group * depth, quarter),
            "req",
            axis=0,
            tiled=True,
            axis_index_groups=members,
        )
        for m in range(3)
    ]

    rim = lax.ppermute(gathered[rows - RIM :], "req", [(i, i + 1) for i in range(n - 1)])
    token_rows = gathered.astype(F32)
    normed = rms_scale(token_rows, in_gain).astype(BF16)
    gate_lin = mm(normed, w_gate).astype(BF16)
    small = mm(normed, jnp.concatenate([w_beta, w_decay], axis=1))
    rim_normed = rms_scale(rim.astype(F32), in_gain).astype(BF16)
    ext = jnp.concatenate([rim_normed, normed], axis=0)
    pq = mm(ext, w_query).astype(BF16)
    pk = mm(ext, w_key).astype(BF16)
    pv = mm(ext, w_value).astype(BF16)

    beta = jax.nn.sigmoid(small[:, :heads]).T
    gdec = (-jnp.exp(decay_log) * jax.nn.softplus(small[:, heads:] + decay_bias)).T
    piece_start = me * rows
    reach = piece_start - (taps - 1) + jnp.arange(rows + taps - 1, dtype=jnp.int32)
    seg_all = segment_of(reach, lengths)
    seg = seg_all[taps - 1 :]
    seg_chunks = seg.reshape(count, chunk)
    prior = segment_of(
        piece_start + jnp.arange(count, dtype=jnp.int32) * chunk - 1, lengths
    )
    opened = (seg_chunks == prior[:, None]).astype(F32)
    to_last = (seg_chunks == seg_chunks[:, -1:]).astype(F32)
    upper = jnp.triu(jnp.ones((chunk, chunk), F32))
    cum = jnp.dot(
        gdec.reshape(heads * count, chunk), upper, precision=lax.Precision.HIGHEST
    ).reshape(heads, count, chunk)
    start_decay = jnp.exp(cum) * opened[None]
    final_w = jnp.exp(cum[:, :, -1:] - cum) * to_last[None]
    carry = jnp.broadcast_to(start_decay[:, :, -1:], cum.shape)

    def shared(a):
        return jnp.broadcast_to(a.astype(F32)[None], (heads, rows))

    fields = [beta] + [a.reshape(heads, rows) for a in (cum, start_decay, final_w, carry)]
    fields.append(shared(seg))
    fields += [
        shared(seg_all[taps - 1 - s : taps - 1 - s + rows] == seg) for s in range(1, taps)
    ]
    fields.append(jnp.zeros(((16 - len(fields)) * heads, rows), F32))
    scal = jnp.transpose(
        lax.optimization_barrier(jnp.concatenate(fields, axis=0)).reshape(16, heads, rows),
        (1, 0, 2),
    )
    qeff, oloc, maps = local_maps(
        pq, pk, pv, conv_query, conv_key, conv_value, scal, chunk, 2
    )
    states = chain_states(maps, n)
    head_out = finish_heads(qeff, oloc, states, gate_lin, head_gain, 2)
    partial_out = mm(head_out, w_out)
    if lax.axis_size("mlp") > 1:
        partial_out = lax.psum(partial_out.astype(BF16), "mlp").astype(F32)
    resid = token_rows + partial_out
    mlp_in = rms_scale(resid, mlp_gain).astype(BF16)
    far_b = swapped(mlp_in, n, 2)
    near = jnp.concatenate([mlp_in, swapped(mlp_in, n, 1)], axis=0)
    far = jnp.concatenate([far_b, swapped(far_b, n, 1)], axis=0)

    def hidden_of(x):
        return (jax.nn.silu(mm(x, up_gate_part)) * mm(x, up_part)).astype(BF16)

    near_hidden = hidden_of(near)
    far_down = mm_t(hidden_of(far), down_part)
    far_chip = far_down[:rows] + swapped(far_down[rows:].astype(BF16), n, 1).astype(F32)
    from_far = swapped(far_chip.astype(BF16), n, 2).astype(F32)
    near_down = mm_t(near_hidden, down_part)
    from_near = swapped(near_down[rows:].astype(BF16), n, 1).astype(F32)
    down = near_down[:rows] + from_near + from_far
    if lax.axis_size("mlp") > 1:
        down = lax.psum_scatter(
            down.astype(BF16), "mlp", scatter_dimension=0, tiled=True
        ).astype(F32)
        resid = lax.dynamic_slice_in_dim(
            resid, lax.axis_index("mlp") * share_rows, share_rows, 0
        )
    return (resid + down).astype(BF16)


def solution(mesh):
    placed = (
        P(("req", "mlp"), None),
        P(),
        P(),
        P(None, "mlp"),
        P(None, "mlp"),
        P(None, "mlp"),
        P(None, "mlp"),
        P(None, "mlp"),
        P(None, "mlp"),
        P("mlp"),
        P("mlp"),
        P(None, "mlp"),
        P(None, "mlp"),
        P(None, "mlp"),
        P(),
        P("mlp", None),
        P(),
        P("req", "mlp"),
        P("req", "mlp"),
        P("mlp", "req"),
    )
    return jax.shard_map(
        per_device, mesh=mesh, in_specs=placed, out_specs=P(("req", "mlp"), None), check_vma=False
    )
```

```python
import functools
import jax
import jax.numpy as jnp
from jax import lax
from jax.experimental import pallas as pl
from jax.experimental.pallas import tpu as pltpu
from jax.sharding import PartitionSpec as P

RIM = 16
F32 = jnp.float32
BF16 = jnp.bfloat16


def rms_scale(values, gain):
    mean_square = jnp.mean(values * values, axis=-1, keepdims=True)
    return values / jnp.sqrt(mean_square + 1e-06) * gain


def segment_of(positions, lengths):
    bounds = jnp.cumsum(lengths)[:-1]
    return jnp.sum((positions[:, None] >= bounds[None, :]).astype(jnp.int32), axis=1)


def mm(a, b):
    return jnp.dot(a, b, preferred_element_type=F32)


def mm_t(a, b):
    return lax.dot_general(a, b, (((1,), (1,)), ((), ())), preferred_element_type=F32)


def split(a):
    high = a.astype(BF16)
    return high, (a - high.astype(F32)).astype(BF16)


def mm3(a, b):
    ah, al = a
    bh, bl = b
    return mm(ah, bh) + (mm(ah, bl) + mm(al, bh))


def conv_silu(p_ref, taps_ref, lanes, scratch, masks, rows):
    scratch[...] = p_ref[:, lanes].astype(F32)
    taps = taps_ref.shape[0]
    acc = None
    for i in range(taps):
        back = taps - 1 - i
        window = scratch[pl.ds(RIM - back, rows), :]
        term = taps_ref[i : i + 1, lanes] * window
        if back:
            term = term * masks[back - 1]
        acc = term if acc is None else acc + term
    return acc / (1.0 + jnp.exp(-acc))


def local_kernel(
    chunk, dk, dv, pq, pk, pv, tq, tk, tv, scal, qeff, oloc, maps, scr_q, scr_k, scr_v
):
    heads = scal.shape[0]
    rows = scal.shape[2]
    count = rows // chunk
    row_i = lax.broadcasted_iota(jnp.int32, (chunk, chunk), 0)
    col_i = lax.broadcasted_iota(jnp.int32, (chunk, chunk), 1)
    eye = (row_i == col_i).astype(F32)
    pairs = [(h, c) for h in range(heads) for c in range(count)]
    cols, lanes, keys, queries, values = [], [], [], [], []
    for h in range(heads):
        lane = scal[h]
        col = lane.T
        masks = [col[:, 6 + s : 7 + s] for s in range(3)]
        q = conv_silu(pq, tq, slice(h * dk, (h + 1) * dk), scr_q.at[h], masks, rows)
        k = conv_silu(pk, tk, slice(h * dk, (h + 1) * dk), scr_k.at[h], masks, rows)
        v = conv_silu(pv, tv, slice(h * dv, (h + 1) * dv), scr_v.at[h], masks, rows)
        q = q * (lax.rsqrt(jnp.sum(q * q, axis=-1, keepdims=True) + 1e-06) * dk ** (-0.5))
        k = k * lax.rsqrt(jnp.sum(k * k, axis=-1, keepdims=True) + 1e-06)
        cols.append(col)
        lanes.append(lane)
        queries.append(q.astype(BF16))
        keys.append(k.astype(BF16))
        values.append(v * col[:, 0:1])
    lower, attend, inverse = {}, {}, {}
    for h, c in pairs:
        part = slice(c * chunk, (c + 1) * chunk)
        col, lane = cols[h][part], lanes[h][:, part]
        kb, qb = keys[h][part], queries[h][part]
        keep = (row_i >= col_i) & (col[:, 5:6] == lane[5:6, :])
        gaps = col[:, 1:2] - lane[1:2, :]
        weights = jnp.where(keep, jnp.exp(jnp.where(keep, gaps, 0.0)), 0.0)
        dots = mm_t(jnp.concatenate([kb, qb], axis=0), kb)
        lower[h, c] = jnp.where(row_i > col_i, col[:, 0:1] * weights * dots[:chunk], 0.0)
        attend[h, c] = (weights * dots[chunk:]).astype(BF16)
    shift = 0
    while (1 << shift) < chunk:
        level = ((row_i >> shift) != (col_i >> shift)) & (
            (row_i >> (shift + 1)) == (col_i >> (shift + 1))
        )
        if shift == 0:
            for p in pairs:
                inverse[p] = eye - jnp.where(level, lower[p], 0.0)
        else:
            halves = {p: split(inverse[p]) for p in pairs}
            mid = {p: mm3(halves[p], split(jnp.where(level, lower[p], 0.0))) for p in pairs}
            for p in pairs:
                inverse[p] = inverse[p] - mm3(split(mid[p]), halves[p])
        shift += 1
    start = jnp.concatenate(
        [
            (
                lax.broadcasted_iota(jnp.int32, (dk, dk), 0)
                == lax.broadcasted_iota(jnp.int32, (dk, dk), 1)
            ).astype(F32),
            jnp.zeros((dk, dv), F32),
        ],
        axis=1,
    )
    state = [start for _ in range(heads)]
    for c in range(count):
        part = slice(c * chunk, (c + 1) * chunk)
        for h in range(heads):
            col, lane = cols[h][part], lanes[h][:, part]
            kb, qb = keys[h][part], queries[h][part]
            sd = col[:, 2:3]
            both = mm(jnp.concatenate([kb, qb], axis=0), state[h].astype(BF16))
            fresh = jnp.concatenate(
                [jnp.zeros((chunk, dk), F32), values[h][part]], axis=1
            ) - (col[:, 0:1] * sd) * both[:chunk]
            update = mm(inverse[h, c].astype(BF16), fresh.astype(BF16))
            out = sd * both[chunk:] + mm(attend[h, c], update.astype(BF16))
            qeff[h, part, :] = out[:, :dk].astype(BF16)
            oloc[h, part, :] = out[:, dk:].astype(BF16)
            final = (col[:, 3:4] * update).astype(BF16)
            state[h] = lane[4:5, 0:1] * state[h] + mm(kb.astype(F32).T.astype(BF16), final)
    for h in range(heads):
        maps[h] = state[h].astype(BF16)


def local_maps(pq, pk, pv, tq, tk, tv, scal, chunk, per_step):
    heads, extra, rows = scal.shape
    dk, dv = pq.shape[1] // heads, pv.shape[1] // heads
    ext = pq.shape[0]
    by_lane = lambda r, w: pl.BlockSpec((r, w * per_step), lambda g: (0, g))
    by_head = lambda r, w: pl.BlockSpec((per_step, r, w), lambda g: (g, 0, 0))
    taps = tq.shape[0]
    return pl.pallas_call(
        functools.partial(local_kernel, chunk, dk, dv),
        grid=(heads // per_step,),
        in_specs=[
            by_lane(ext, dk),
            by_lane(ext, dk),
            by_lane(ext, dv),
            by_lane(taps, dk),
            by_lane(taps, dk),
            by_lane(taps, dv),
            by_head(extra, rows),
        ],
        out_specs=[by_head(rows, dk), by_head(rows, dv), by_head(dk, dk + dv)],
        out_shape=[
            jax.ShapeDtypeStruct((heads, rows, dk), BF16),
            jax.ShapeDtypeStruct((heads, rows, dv), BF16),
            jax.ShapeDtypeStruct((heads, dk, dk + dv), BF16),
        ],
        scratch_shapes=[
            pltpu.VMEM((per_step, ext, dk), F32),
            pltpu.VMEM((per_step, ext, dk), F32),
            pltpu.VMEM((per_step, ext, dv), F32),
        ],
        compiler_params=pltpu.CompilerParams(vmem_limit_bytes=48 * 2**20),
        cost_estimate=pl.CostEstimate(
            flops=10**9, bytes_accessed=20 * 2**20, transcendentals=0
        ),
        name="local_maps",
    )(pq, pk, pv, tq, tk, tv, scal)


def chain_kernel(
    n, dk, maps, states, theirs, first, joined, landing, outgoing, to_peer, from_peer,
    swap_send, swap_recv, send_sem, recv_sem, peer_send, peer_recv
):
    me = lax.axis_index("req")
    core = lax.rem(me, 2)
    peer = me + 1 - 2 * core
    per_core = joined.shape[0]
    has_left, has_right = me >= 2, me < n - 2
    barrier = pltpu.get_barrier_semaphore()
    mesh_id = pl.DeviceIdType.MESH
    pl.semaphore_signal(barrier, inc=1, device_id={"req": peer}, device_id_type=mesh_id)

    @pl.when(has_left)
    def _():
        pl.semaphore_signal(barrier, inc=1, device_id={"req": me - 2}, device_id_type=mesh_id)

    pl.semaphore_wait(barrier, 1 + has_right.astype(jnp.int32))
    own_base = core * per_core
    peer_base = (1 - core) * per_core

    swap = pltpu.make_async_remote_copy(
        src_ref=maps.at[pl.ds(peer_base, per_core)],
        dst_ref=theirs,
        send_sem=swap_send,
        recv_sem=swap_recv,
        device_id={"req": peer},
        device_id_type=mesh_id,
    )
    swap.start()
    swap.wait_recv()

    def join(h, carry):
        mine, other = maps[own_base + h], theirs[h]
        early = jnp.where(core == 0, mine, other)
        late = jnp.where(core == 0, other, mine)
        both = mm(late[:, :dk], early)
        first[h] = early
        joined[h, :, :dk] = both[:, :dk].astype(BF16)
        joined[h, :, dk:] = (both[:, dk:] + late[:, dk:].astype(F32)).astype(BF16)
        return carry

    lax.fori_loop(0, per_core, join, 0)

    def onward_copy(h, part):
        return pltpu.make_async_remote_copy(
            src_ref=outgoing.at[part, h],
            dst_ref=landing.at[part, h],
            send_sem=send_sem.at[part, h],
            recv_sem=recv_sem.at[part, h],
            device_id={"req": me + 2},
            device_id_type=mesh_id,
        )

    def peer_copy(h):
        return pltpu.make_async_remote_copy(
            src_ref=to_peer.at[h],
            dst_ref=from_peer.at[h],
            send_sem=peer_send.at[h],
            recv_sem=peer_recv.at[h],
            device_id={"req": peer},
            device_id_type=mesh_id,
        )

    parts = landing.shape[0]
    width = landing.shape[3]

    def one(h, carry):
        for part in range(parts):
            lanes = slice(dk + part * width, dk + (part + 1) * width)

            @pl.when(has_left)
            def _():
                onward_copy(h, part).wait_recv()

            @pl.when(jnp.logical_not(has_left))
            def _():
                landing[part, h] = jnp.zeros(landing.shape[2:], BF16)

            @pl.when(has_right)
            def _():
                onward = mm(joined[h, :, :dk], landing[part, h])
                outgoing[part, h] = (onward + joined[h, :, lanes].astype(F32)).astype(BF16)
                onward_copy(h, part).start()

        coming = jnp.concatenate([landing[part, h] for part in range(parts)], axis=1)
        middle = (mm(first[h, :, :dk], coming) + first[h, :, dk:].astype(F32)).astype(BF16)
        states[own_base + h] = jnp.where(core == 0, coming, middle)
        to_peer[h] = jnp.where(core == 0, middle, coming)
        peer_copy(h).start()
        return carry

    lax.fori_loop(0, per_core, one, 0)

    def collect(h, carry):
        peer_copy(h).wait_recv()
        states[peer_base + h] = from_peer[h]
        peer_copy(h).wait_send()
        return carry

    lax.fori_loop(0, per_core, collect, 0)

    def drain(h, carry):
        for part in range(parts):
            onward_copy(h, part).wait_send()
        return carry

    @pl.when(has_right)
    def _():
        lax.fori_loop(0, per_core, drain, 0)

    swap.wait_send()


def chain_states(maps, n):
    heads, dk, width = maps.shape
    dv = width - dk
    per_core = heads // 2
    map_buf = pltpu.VMEM((per_core, dk, width), BF16)
    state_buf = pltpu.VMEM((per_core, dk, dv), BF16)
    parts = dv // 128 if dv % 128 == 0 else 1
    part_buf = pltpu.VMEM((parts, per_core, dk, dv // parts), BF16)
    sems = pltpu.SemaphoreType.DMA((per_core,))
    part_sems = pltpu.SemaphoreType.DMA((parts, per_core))
    return pl.pallas_call(
        functools.partial(chain_kernel, n, dk),
        in_specs=[pl.BlockSpec(memory_space=pltpu.VMEM)],
        out_specs=pl.BlockSpec(memory_space=pltpu.VMEM),
        out_shape=jax.ShapeDtypeStruct((heads, dk, dv), BF16),
        scratch_shapes=[map_buf] * 3
        + [part_buf] * 2
        + [state_buf] * 2
        + [pltpu.SemaphoreType.DMA] * 2
        + [part_sems] * 2
        + [sems] * 2,
        compiler_params=pltpu.CompilerParams(
            collective_id=0, has_side_effects=True, vmem_limit_bytes=32 * 2**20
        ),
        cost_estimate=pl.CostEstimate(
            flops=10**9, bytes_accessed=3 * 2**20, transcendentals=0
        ),
        name="chain_states",
    )(maps)


def finish_kernel(qeff, oloc, states, gate, gain, out):
    heads, dv = oloc.shape[0], oloc.shape[2]
    for h in range(heads):
        lanes = slice(h * dv, (h + 1) * dv)
        rec = mm(qeff[h], states[h]) + oloc[h].astype(F32)
        rec = rec * lax.rsqrt(jnp.mean(rec * rec, axis=-1, keepdims=True) + 1e-06)
        g = gate[:, lanes].astype(F32)
        out[:, lanes] = (rec * gain[...] * (g / (1.0 + jnp.exp(-g)))).astype(BF16)


def finish_heads(qeff, oloc, states, gate, gain, per_step):
    heads, rows, dk = qeff.shape
    dv = oloc.shape[2]
    by_head = lambda r, w: pl.BlockSpec((per_step, r, w), lambda g: (g, 0, 0))
    lane = pl.BlockSpec((rows, dv * per_step), lambda g: (0, g))
    return pl.pallas_call(
        finish_kernel,
        grid=(heads // per_step,),
        in_specs=[
            by_head(rows, dk),
            by_head(rows, dv),
            by_head(dk, dv),
            lane,
            pl.BlockSpec((1, dv), lambda g: (0, 0)),
        ],
        out_specs=lane,
        out_shape=jax.ShapeDtypeStruct((rows, heads * dv), BF16),
        compiler_params=pltpu.CompilerParams(vmem_limit_bytes=32 * 2**20),
        cost_estimate=pl.CostEstimate(
            flops=2 * heads * rows * dk * dv, bytes_accessed=12 * 2**20, transcendentals=0
        ),
        name="finish_heads",
    )(qeff, oloc, states, gate, gain.reshape(1, dv))


def zero_after(value):
    return jnp.minimum(jnp.abs(value[0, 0].astype(F32)), 0.0).astype(jnp.int32)


def swapped(value, n, bits):
    return lax.ppermute(value, "req", [(i, i ^ bits) for i in range(n)])


def per_device(
    tokens,
    lengths,
    in_gain,
    w_query,
    w_key,
    w_value,
    w_gate,
    w_beta,
    w_decay,
    decay_log,
    decay_bias,
    conv_query,
    conv_key,
    conv_value,
    head_gain,
    w_out,
    mlp_gain,
    w_up_gate,
    w_up,
    w_down,
):
    n = lax.axis_size("req")
    me = lax.axis_index("req")
    share_rows = tokens.shape[0]
    gathered = lax.all_gather(tokens, "mlp", axis=0, tiled=True)
    rows = gathered.shape[0]
    heads = w_beta.shape[1]
    taps = conv_query.shape[0]
    chunk = 128
    count = rows // chunk
    token_rows = gathered.astype(F32)
    normed = rms_scale(token_rows, in_gain).astype(BF16)
    gate_lin = mm(normed, w_gate).astype(BF16)
    group = 4
    spot = me % group
    quarter = w_up.shape[1] // group
    shards = jnp.concatenate([w_up_gate, w_up, w_down.T], axis=0)
    depth = w_up.shape[0]
    pieces = jnp.zeros((group,) + (shards.shape[0], quarter), BF16)
    received = []
    for d in range(group):
        piece = lax.dynamic_slice_in_dim(shards, (spot ^ d) * quarter, quarter, 1)
        received.append(swapped(piece, n, d) if d else piece)
    gated = zero_after(gate_lin)
    for d in range(group):
        place = (spot ^ d) + (gated if d else 0)
        pieces = lax.dynamic_update_slice_in_dim(pieces, received[d][None], place, 0)
    members = [list(range(k, n, group)) for k in range(group)]
    blocks = [
        pieces[:, m * depth : (m + 1) * depth].reshape(group * depth, quarter)
        for m in range(3)
    ]
    mlp_part = lax.all_gather(
        jnp.concatenate(blocks, axis=1),
        "req",
        axis=0,
        tiled=True,
        axis_index_groups=members,
    )
    rim = lax.ppermute(gathered[rows - RIM :], "req", [(i, i + 1) for i in range(n - 1)])
    small = mm(normed, jnp.concatenate([w_beta, w_decay], axis=1))
    rim = rim.astype(F32) + zero_after(pieces[0]).astype(F32)
    rim_normed = rms_scale(rim, in_gain).astype(BF16)
    ext = jnp.concatenate([rim_normed, normed], axis=0)
    pq = mm(ext, w_query).astype(BF16)
    pk = mm(ext, w_key).astype(BF16)
    pv = mm(ext, w_value).astype(BF16)

    beta = jax.nn.sigmoid(small[:, :heads]).T
    gdec = (-jnp.exp(decay_log) * jax.nn.softplus(small[:, heads:] + decay_bias)).T
    piece_start = me * rows
    reach = piece_start - (taps - 1) + jnp.arange(rows + taps - 1, dtype=jnp.int32)
    seg_all = segment_of(reach, lengths)
    seg = seg_all[taps - 1 :]
    seg_chunks = seg.reshape(count, chunk)
    prior = segment_of(
        piece_start + jnp.arange(count, dtype=jnp.int32) * chunk - 1, lengths
    )
    opened = (seg_chunks == prior[:, None]).astype(F32)
    to_last = (seg_chunks == seg_chunks[:, -1:]).astype(F32)
    upper = jnp.triu(jnp.ones((chunk, chunk), F32))
    cum = jnp.dot(
        gdec.reshape(heads * count, chunk), upper, precision=lax.Precision.HIGHEST
    ).reshape(heads, count, chunk)
    start_decay = jnp.exp(cum) * opened[None]
    final_w = jnp.exp(cum[:, :, -1:] - cum) * to_last[None]
    carry = jnp.broadcast_to(start_decay[:, :, -1:], cum.shape)

    def shared(a):
        return jnp.broadcast_to(a.astype(F32)[None], (heads, rows))

    fields = [beta] + [a.reshape(heads, rows) for a in (cum, start_decay, final_w, carry)]
    fields.append(shared(seg))
    fields += [
        shared(seg_all[taps - 1 - s : taps - 1 - s + rows] == seg) for s in range(1, taps)
    ]
    fields.append(jnp.zeros(((16 - len(fields)) * heads, rows), F32))
    scal = jnp.transpose(
        lax.optimization_barrier(jnp.concatenate(fields, axis=0)).reshape(16, heads, rows),
        (1, 0, 2),
    )
    qeff, oloc, maps = local_maps(
        pq, pk, pv, conv_query, conv_key, conv_value, scal, chunk, 2
    )
    states = chain_states(maps, n)
    head_out = finish_heads(qeff, oloc, states, gate_lin, head_gain, 2)
    partial_out = mm(head_out, w_out)
    if lax.axis_size("mlp") > 1:
        partial_out = lax.psum(partial_out.astype(BF16), "mlp").astype(F32)
    resid = token_rows + partial_out
    mlp_in = rms_scale(resid, mlp_gain).astype(BF16)
    up_part, down_part = mlp_part[:, : 2 * quarter], mlp_part[:, 2 * quarter :]
    far_b = swapped(mlp_in, n, 2)
    near = jnp.concatenate([mlp_in, swapped(mlp_in, n, 1)], axis=0)
    far = jnp.concatenate([far_b, swapped(far_b, n, 1)], axis=0)

    def swiglu(x):
        acc = mm(x, up_part)
        hidden = (jax.nn.silu(acc[:, :quarter]) * acc[:, quarter:]).astype(BF16)
        return mm_t(hidden, down_part)

    far_down = swiglu(far)
    far_chip = far_down[:rows] + swapped(far_down[rows:].astype(BF16), n, 1).astype(F32)
    far_chip = far_chip.astype(BF16)
    from_far = swapped(far_chip, n, 2).astype(F32)
    near_down = swiglu(near + zero_after(far_chip).astype(BF16))
    near_send = near_down[rows:] + zero_after(from_far).astype(F32)
    from_near = swapped(near_send.astype(BF16), n, 1).astype(F32)
    down = near_down[:rows] + from_near + from_far
    if lax.axis_size("mlp") > 1:
        down = lax.psum_scatter(
            down.astype(BF16), "mlp", scatter_dimension=0, tiled=True
        ).astype(F32)
        resid = lax.dynamic_slice_in_dim(
            resid, lax.axis_index("mlp") * share_rows, share_rows, 0
        )
    return (resid + down).astype(BF16)


def solution(mesh):
    placed = (
        P(("req", "mlp"), None),
        P(),
        P(),
        P(None, "mlp"),
        P(None, "mlp"),
        P(None, "mlp"),
        P(None, "mlp"),
        P(None, "mlp"),
        P(None, "mlp"),
        P("mlp"),
        P("mlp"),
        P(None, "mlp"),
        P(None, "mlp"),
        P(None, "mlp"),
        P(),
        P("mlp", None),
        P(),
        P("req", "mlp"),
        P("req", "mlp"),
        P("mlp", "req"),
    )
    return jax.shard_map(
        per_device, mesh=mesh, in_specs=placed, out_specs=P(("req", "mlp"), None), check_vma=False
    )
```

```python
import functools
import jax
import jax.numpy as jnp
from jax import lax
from jax.experimental import pallas as pl
from jax.experimental.pallas import tpu as pltpu
from jax.sharding import PartitionSpec as P

RIM = 16
F32 = jnp.float32
BF16 = jnp.bfloat16


def rms_scale(values, gain):
    mean_square = jnp.mean(values * values, axis=-1, keepdims=True)
    return values / jnp.sqrt(mean_square + 1e-06) * gain


def segment_of(positions, lengths):
    bounds = jnp.cumsum(lengths)[:-1]
    return jnp.sum((positions[:, None] >= bounds[None, :]).astype(jnp.int32), axis=1)


def mm(a, b):
    return jnp.dot(a, b, preferred_element_type=F32)


def mm_t(a, b):
    return lax.dot_general(a, b, (((1,), (1,)), ((), ())), preferred_element_type=F32)


def split(a):
    high = a.astype(BF16)
    return high, (a - high.astype(F32)).astype(BF16)


def mm3(a, b):
    ah, al = a
    bh, bl = b
    return mm(ah, bh) + (mm(ah, bl) + mm(al, bh))


def conv_silu(p_ref, taps_ref, lanes, scratch, masks, rows):
    scratch[...] = p_ref[:, lanes].astype(F32)
    taps = taps_ref.shape[0]
    acc = None
    for i in range(taps):
        back = taps - 1 - i
        window = scratch[pl.ds(RIM - back, rows), :]
        term = taps_ref[i : i + 1, lanes] * window
        if back:
            term = term * masks[back - 1]
        acc = term if acc is None else acc + term
    return acc / (1.0 + jnp.exp(-acc))


def local_kernel(
    chunk, dk, dv, pq, pk, pv, tq, tk, tv, scal, qeff, oloc, maps, scr_q, scr_k, scr_v
):
    heads = scal.shape[0]
    rows = scal.shape[2]
    count = rows // chunk
    row_i = lax.broadcasted_iota(jnp.int32, (chunk, chunk), 0)
    col_i = lax.broadcasted_iota(jnp.int32, (chunk, chunk), 1)
    eye = (row_i == col_i).astype(F32)
    pairs = [(h, c) for h in range(heads) for c in range(count)]
    cols, lanes, keys, queries, values = [], [], [], [], []
    for h in range(heads):
        lane = scal[h]
        col = lane.T
        masks = [col[:, 6 + s : 7 + s] for s in range(3)]
        q = conv_silu(pq, tq, slice(h * dk, (h + 1) * dk), scr_q.at[h], masks, rows)
        k = conv_silu(pk, tk, slice(h * dk, (h + 1) * dk), scr_k.at[h], masks, rows)
        v = conv_silu(pv, tv, slice(h * dv, (h + 1) * dv), scr_v.at[h], masks, rows)
        q = q * (lax.rsqrt(jnp.sum(q * q, axis=-1, keepdims=True) + 1e-06) * dk ** (-0.5))
        k = k * lax.rsqrt(jnp.sum(k * k, axis=-1, keepdims=True) + 1e-06)
        cols.append(col)
        lanes.append(lane)
        queries.append(q.astype(BF16))
        keys.append(k.astype(BF16))
        values.append(v * col[:, 0:1])
    lower, attend, inverse = {}, {}, {}
    for h, c in pairs:
        part = slice(c * chunk, (c + 1) * chunk)
        col, lane = cols[h][part], lanes[h][:, part]
        kb, qb = keys[h][part], queries[h][part]
        keep = (row_i >= col_i) & (col[:, 5:6] == lane[5:6, :])
        gaps = col[:, 1:2] - lane[1:2, :]
        weights = jnp.where(keep, jnp.exp(jnp.where(keep, gaps, 0.0)), 0.0)
        dots = mm_t(jnp.concatenate([kb, qb], axis=0), kb)
        lower[h, c] = jnp.where(row_i > col_i, col[:, 0:1] * weights * dots[:chunk], 0.0)
        attend[h, c] = (weights * dots[chunk:]).astype(BF16)
    shift = 0
    while (1 << shift) < chunk:
        level = ((row_i >> shift) != (col_i >> shift)) & (
            (row_i >> (shift + 1)) == (col_i >> (shift + 1))
        )
        if shift == 0:
            for p in pairs:
                inverse[p] = eye - jnp.where(level, lower[p], 0.0)
        else:
            halves = {p: split(inverse[p]) for p in pairs}
            mid = {p: mm3(halves[p], split(jnp.where(level, lower[p], 0.0))) for p in pairs}
            for p in pairs:
                inverse[p] = inverse[p] - mm3(split(mid[p]), halves[p])
        shift += 1
    start = jnp.concatenate(
        [
            (
                lax.broadcasted_iota(jnp.int32, (dk, dk), 0)
                == lax.broadcasted_iota(jnp.int32, (dk, dk), 1)
            ).astype(F32),
            jnp.zeros((dk, dv), F32),
        ],
        axis=1,
    )
    state = [start for _ in range(heads)]
    for c in range(count):
        part = slice(c * chunk, (c + 1) * chunk)
        for h in range(heads):
            col, lane = cols[h][part], lanes[h][:, part]
            kb, qb = keys[h][part], queries[h][part]
            sd = col[:, 2:3]
            both = mm(jnp.concatenate([kb, qb], axis=0), state[h].astype(BF16))
            fresh = jnp.concatenate(
                [jnp.zeros((chunk, dk), F32), values[h][part]], axis=1
            ) - (col[:, 0:1] * sd) * both[:chunk]
            update = mm(inverse[h, c].astype(BF16), fresh.astype(BF16))
            out = sd * both[chunk:] + mm(attend[h, c], update.astype(BF16))
            qeff[h, part, :] = out[:, :dk].astype(BF16)
            oloc[h, part, :] = out[:, dk:].astype(BF16)
            final = (col[:, 3:4] * update).astype(BF16)
            state[h] = lane[4:5, 0:1] * state[h] + mm(kb.astype(F32).T.astype(BF16), final)
    for h in range(heads):
        maps[h] = state[h].astype(BF16)


def local_maps(pq, pk, pv, tq, tk, tv, scal, chunk, per_step):
    heads, extra, rows = scal.shape
    dk, dv = pq.shape[1] // heads, pv.shape[1] // heads
    ext = pq.shape[0]
    by_lane = lambda r, w: pl.BlockSpec((r, w * per_step), lambda g: (0, g))
    by_head = lambda r, w: pl.BlockSpec((per_step, r, w), lambda g: (g, 0, 0))
    taps = tq.shape[0]
    return pl.pallas_call(
        functools.partial(local_kernel, chunk, dk, dv),
        grid=(heads // per_step,),
        in_specs=[
            by_lane(ext, dk),
            by_lane(ext, dk),
            by_lane(ext, dv),
            by_lane(taps, dk),
            by_lane(taps, dk),
            by_lane(taps, dv),
            by_head(extra, rows),
        ],
        out_specs=[by_head(rows, dk), by_head(rows, dv), by_head(dk, dk + dv)],
        out_shape=[
            jax.ShapeDtypeStruct((heads, rows, dk), BF16),
            jax.ShapeDtypeStruct((heads, rows, dv), BF16),
            jax.ShapeDtypeStruct((heads, dk, dk + dv), BF16),
        ],
        scratch_shapes=[
            pltpu.VMEM((per_step, ext, dk), F32),
            pltpu.VMEM((per_step, ext, dk), F32),
            pltpu.VMEM((per_step, ext, dv), F32),
        ],
        compiler_params=pltpu.CompilerParams(vmem_limit_bytes=48 * 2**20),
        cost_estimate=pl.CostEstimate(
            flops=10**9, bytes_accessed=20 * 2**20, transcendentals=0
        ),
        name="local_maps",
    )(pq, pk, pv, tq, tk, tv, scal)


def chain_kernel(
    n, dk, maps, states, theirs, first, joined, landing, outgoing, to_peer, from_peer,
    swap_send, swap_recv, send_sem, recv_sem, peer_send, peer_recv
):
    me = lax.axis_index("req")
    core = lax.rem(me, 2)
    peer = me + 1 - 2 * core
    per_core = joined.shape[0]
    has_left, has_right = me >= 2, me < n - 2
    barrier = pltpu.get_barrier_semaphore()
    mesh_id = pl.DeviceIdType.MESH
    pl.semaphore_signal(barrier, inc=1, device_id={"req": peer}, device_id_type=mesh_id)

    @pl.when(has_left)
    def _():
        pl.semaphore_signal(barrier, inc=1, device_id={"req": me - 2}, device_id_type=mesh_id)

    pl.semaphore_wait(barrier, 1 + has_right.astype(jnp.int32))
    own_base = core * per_core
    peer_base = (1 - core) * per_core

    swap = pltpu.make_async_remote_copy(
        src_ref=maps.at[pl.ds(peer_base, per_core)],
        dst_ref=theirs,
        send_sem=swap_send,
        recv_sem=swap_recv,
        device_id={"req": peer},
        device_id_type=mesh_id,
    )
    swap.start()
    swap.wait_recv()

    def join(h, carry):
        mine, other = maps[own_base + h], theirs[h]
        early = jnp.where(core == 0, mine, other)
        late = jnp.where(core == 0, other, mine)
        both = mm(late[:, :dk], early)
        first[h] = early
        joined[h, :, :dk] = both[:, :dk].astype(BF16)
        joined[h, :, dk:] = (both[:, dk:] + late[:, dk:].astype(F32)).astype(BF16)
        return carry

    lax.fori_loop(0, per_core, join, 0)

    def onward_copy(h, part):
        return pltpu.make_async_remote_copy(
            src_ref=outgoing.at[part, h],
            dst_ref=landing.at[part, h],
            send_sem=send_sem.at[part, h],
            recv_sem=recv_sem.at[part, h],
            device_id={"req": me + 2},
            device_id_type=mesh_id,
        )

    def peer_copy(h):
        return pltpu.make_async_remote_copy(
            src_ref=to_peer.at[h],
            dst_ref=from_peer.at[h],
            send_sem=peer_send.at[h],
            recv_sem=peer_recv.at[h],
            device_id={"req": peer},
            device_id_type=mesh_id,
        )

    parts = landing.shape[0]
    width = landing.shape[3]

    def one(h, carry):
        for part in range(parts):
            lanes = slice(dk + part * width, dk + (part + 1) * width)

            @pl.when(has_left)
            def _():
                onward_copy(h, part).wait_recv()

            @pl.when(jnp.logical_not(has_left))
            def _():
                landing[part, h] = jnp.zeros(landing.shape[2:], BF16)

            @pl.when(has_right)
            def _():
                onward = mm(joined[h, :, :dk], landing[part, h])
                outgoing[part, h] = (onward + joined[h, :, lanes].astype(F32)).astype(BF16)
                onward_copy(h, part).start()

        coming = jnp.concatenate([landing[part, h] for part in range(parts)], axis=1)
        middle = (mm(first[h, :, :dk], coming) + first[h, :, dk:].astype(F32)).astype(BF16)
        states[own_base + h] = jnp.where(core == 0, coming, middle)
        to_peer[h] = jnp.where(core == 0, middle, coming)
        peer_copy(h).start()
        return carry

    lax.fori_loop(0, per_core, one, 0)

    def collect(h, carry):
        peer_copy(h).wait_recv()
        states[peer_base + h] = from_peer[h]
        peer_copy(h).wait_send()
        return carry

    lax.fori_loop(0, per_core, collect, 0)

    def drain(h, carry):
        for part in range(parts):
            onward_copy(h, part).wait_send()
        return carry

    @pl.when(has_right)
    def _():
        lax.fori_loop(0, per_core, drain, 0)

    swap.wait_send()


def chain_states(maps, n):
    heads, dk, width = maps.shape
    dv = width - dk
    per_core = heads // 2
    map_buf = pltpu.VMEM((per_core, dk, width), BF16)
    state_buf = pltpu.VMEM((per_core, dk, dv), BF16)
    parts = dv // 128 if dv % 128 == 0 else 1
    part_buf = pltpu.VMEM((parts, per_core, dk, dv // parts), BF16)
    sems = pltpu.SemaphoreType.DMA((per_core,))
    part_sems = pltpu.SemaphoreType.DMA((parts, per_core))
    return pl.pallas_call(
        functools.partial(chain_kernel, n, dk),
        in_specs=[pl.BlockSpec(memory_space=pltpu.VMEM)],
        out_specs=pl.BlockSpec(memory_space=pltpu.VMEM),
        out_shape=jax.ShapeDtypeStruct((heads, dk, dv), BF16),
        scratch_shapes=[map_buf] * 3
        + [part_buf] * 2
        + [state_buf] * 2
        + [pltpu.SemaphoreType.DMA] * 2
        + [part_sems] * 2
        + [sems] * 2,
        compiler_params=pltpu.CompilerParams(
            collective_id=0, has_side_effects=True, vmem_limit_bytes=32 * 2**20
        ),
        cost_estimate=pl.CostEstimate(
            flops=10**9, bytes_accessed=3 * 2**20, transcendentals=0
        ),
        name="chain_states",
    )(maps)


def finish_kernel(qeff, oloc, states, gate, gain, out):
    heads, dv = oloc.shape[0], oloc.shape[2]
    for h in range(heads):
        lanes = slice(h * dv, (h + 1) * dv)
        rec = mm(qeff[h], states[h]) + oloc[h].astype(F32)
        rec = rec * lax.rsqrt(jnp.mean(rec * rec, axis=-1, keepdims=True) + 1e-06)
        g = gate[:, lanes].astype(F32)
        out[:, lanes] = (rec * gain[...] * (g / (1.0 + jnp.exp(-g)))).astype(BF16)


def finish_heads(qeff, oloc, states, gate, gain, per_step):
    heads, rows, dk = qeff.shape
    dv = oloc.shape[2]
    by_head = lambda r, w: pl.BlockSpec((per_step, r, w), lambda g: (g, 0, 0))
    lane = pl.BlockSpec((rows, dv * per_step), lambda g: (0, g))
    return pl.pallas_call(
        finish_kernel,
        grid=(heads // per_step,),
        in_specs=[
            by_head(rows, dk),
            by_head(rows, dv),
            by_head(dk, dv),
            lane,
            pl.BlockSpec((1, dv), lambda g: (0, 0)),
        ],
        out_specs=lane,
        out_shape=jax.ShapeDtypeStruct((rows, heads * dv), BF16),
        compiler_params=pltpu.CompilerParams(vmem_limit_bytes=32 * 2**20),
        cost_estimate=pl.CostEstimate(
            flops=2 * heads * rows * dk * dv, bytes_accessed=12 * 2**20, transcendentals=0
        ),
        name="finish_heads",
    )(qeff, oloc, states, gate, gain.reshape(1, dv))


def zero_after(value):
    return jnp.minimum(jnp.abs(value[0, 0].astype(F32)), 0.0).astype(jnp.int32)


def swapped(value, n, bits):
    return lax.ppermute(value, "req", [(i, i ^ bits) for i in range(n)])


def per_device(
    tokens,
    lengths,
    in_gain,
    w_query,
    w_key,
    w_value,
    w_gate,
    w_beta,
    w_decay,
    decay_log,
    decay_bias,
    conv_query,
    conv_key,
    conv_value,
    head_gain,
    w_out,
    mlp_gain,
    w_up_gate,
    w_up,
    w_down,
):
    n = lax.axis_size("req")
    me = lax.axis_index("req")
    share_rows = tokens.shape[0]
    gathered = lax.all_gather(tokens, "mlp", axis=0, tiled=True)
    rows = gathered.shape[0]
    heads = w_beta.shape[1]
    taps = conv_query.shape[0]
    chunk = 128
    count = rows // chunk
    token_rows = gathered.astype(F32)
    normed = rms_scale(token_rows, in_gain).astype(BF16)
    gate_lin = mm(normed, w_gate).astype(BF16)
    group = 4
    spot = me % group
    quarter = w_up.shape[1] // group
    shards = jnp.concatenate([w_up_gate, w_up, w_down.T], axis=0)
    depth = w_up.shape[0]
    pieces = jnp.zeros((group,) + (shards.shape[0], quarter), BF16)
    received = []
    for d in range(group):
        piece = lax.dynamic_slice_in_dim(shards, (spot ^ d) * quarter, quarter, 1)
        received.append(swapped(piece, n, d) if d else piece)
    gated = zero_after(gate_lin)
    for d in range(group):
        place = (spot ^ d) + (gated if d else 0)
        pieces = lax.dynamic_update_slice_in_dim(pieces, received[d][None], place, 0)
    members = [list(range(k, n, group)) for k in range(group)]
    blocks = [
        pieces[:, m * depth : (m + 1) * depth].reshape(group * depth, quarter)
        for m in range(3)
    ]
    up_part, down_part = [
        lax.all_gather(block, "req", axis=0, tiled=True, axis_index_groups=members)
        for block in (jnp.concatenate(blocks[:2], axis=1), blocks[2])
    ]

    rim = lax.ppermute(gathered[rows - RIM :], "req", [(i, i + 1) for i in range(n - 1)])
    small = mm(normed, jnp.concatenate([w_beta, w_decay], axis=1))
    rim = rim.astype(F32) + zero_after(pieces[0]).astype(F32)
    rim_normed = rms_scale(rim, in_gain).astype(BF16)
    ext = jnp.concatenate([rim_normed, normed], axis=0)
    pq = mm(ext, w_query).astype(BF16)
    pk = mm(ext, w_key).astype(BF16)
    pv = mm(ext, w_value).astype(BF16)

    beta = jax.nn.sigmoid(small[:, :heads]).T
    gdec = (-jnp.exp(decay_log) * jax.nn.softplus(small[:, heads:] + decay_bias)).T
    piece_start = me * rows
    reach = piece_start - (taps - 1) + jnp.arange(rows + taps - 1, dtype=jnp.int32)
    seg_all = segment_of(reach, lengths)
    seg = seg_all[taps - 1 :]
    seg_chunks = seg.reshape(count, chunk)
    prior = segment_of(
        piece_start + jnp.arange(count, dtype=jnp.int32) * chunk - 1, lengths
    )
    opened = (seg_chunks == prior[:, None]).astype(F32)
    to_last = (seg_chunks == seg_chunks[:, -1:]).astype(F32)
    upper = jnp.triu(jnp.ones((chunk, chunk), F32))
    cum = jnp.dot(
        gdec.reshape(heads * count, chunk), upper, precision=lax.Precision.HIGHEST
    ).reshape(heads, count, chunk)
    start_decay = jnp.exp(cum) * opened[None]
    final_w = jnp.exp(cum[:, :, -1:] - cum) * to_last[None]
    carry = jnp.broadcast_to(start_decay[:, :, -1:], cum.shape)

    def shared(a):
        return jnp.broadcast_to(a.astype(F32)[None], (heads, rows))

    fields = [beta] + [a.reshape(heads, rows) for a in (cum, start_decay, final_w, carry)]
    fields.append(shared(seg))
    fields += [
        shared(seg_all[taps - 1 - s : taps - 1 - s + rows] == seg) for s in range(1, taps)
    ]
    fields.append(jnp.zeros(((16 - len(fields)) * heads, rows), F32))
    scal = jnp.transpose(
        lax.optimization_barrier(jnp.concatenate(fields, axis=0)).reshape(16, heads, rows),
        (1, 0, 2),
    )
    qeff, oloc, maps = local_maps(
        pq, pk, pv, conv_query, conv_key, conv_value, scal, chunk, 2
    )
    states = chain_states(maps, n)
    head_out = finish_heads(qeff, oloc, states, gate_lin, head_gain, 2)
    partial_out = mm(head_out, w_out)
    if lax.axis_size("mlp") > 1:
        partial_out = lax.psum(partial_out.astype(BF16), "mlp").astype(F32)
    resid = token_rows + partial_out
    mlp_in = rms_scale(resid, mlp_gain).astype(BF16)
    far_b = swapped(mlp_in, n, 2)
    near = jnp.concatenate([mlp_in, swapped(mlp_in, n, 1)], axis=0)
    far = jnp.concatenate([far_b, swapped(far_b, n, 1)], axis=0)

    def swiglu(x):
        acc = mm(x, up_part)
        hidden = (jax.nn.silu(acc[:, :quarter]) * acc[:, quarter:]).astype(BF16)
        return mm_t(hidden, down_part)

    far_down = swiglu(far)
    far_chip = far_down[:rows] + swapped(far_down[rows:].astype(BF16), n, 1).astype(F32)
    far_chip = far_chip.astype(BF16)
    from_far = swapped(far_chip, n, 2).astype(F32)
    near_down = swiglu(near + zero_after(far_chip).astype(BF16))
    near_send = near_down[rows:] + zero_after(from_far).astype(F32)
    from_near = swapped(near_send.astype(BF16), n, 1).astype(F32)
    down = near_down[:rows] + from_near + from_far
    if lax.axis_size("mlp") > 1:
        down = lax.psum_scatter(
            down.astype(BF16), "mlp", scatter_dimension=0, tiled=True
        ).astype(F32)
        resid = lax.dynamic_slice_in_dim(
            resid, lax.axis_index("mlp") * share_rows, share_rows, 0
        )
    return (resid + down).astype(BF16)


def solution(mesh):
    placed = (
        P(("req", "mlp"), None),
        P(),
        P(),
        P(None, "mlp"),
        P(None, "mlp"),
        P(None, "mlp"),
        P(None, "mlp"),
        P(None, "mlp"),
        P(None, "mlp"),
        P("mlp"),
        P("mlp"),
        P(None, "mlp"),
        P(None, "mlp"),
        P(None, "mlp"),
        P(),
        P("mlp", None),
        P(),
        P("req", "mlp"),
        P("req", "mlp"),
        P("mlp", "req"),
    )
    return jax.shard_map(
        per_device, mesh=mesh, in_specs=placed, out_specs=P(("req", "mlp"), None), check_vma=False
    )
```
